512 devices in a mesh: mp: 32 (over z, x), ctx: 16 (over y, core).
Axes of the slice: x: 4, y: 8, z: 8, core: 2. Of those that a mesh axis runs over, the one named last changes fastest.
Arguments:
- hidden_act: bfloat16 [16384, 25600], P('ctx', 'mp'), may hold values from -6 to 6
- out_grad: bfloat16 [16384, 5120], P('ctx', 'mp'), may hold values from -6 to 6
- proj_in: bfloat16 [25600, 64], P('mp'), may hold values from -0.0390625 to 0.0390625
- proj_out: bfloat16 [5120, 64], P('mp'), may hold values from -0.078125 to 0.078125
- queries: bfloat16 [8192, 4096], P('mp'), may hold values from -0.09375 to 0.09375
- lengths: int32 [256], replicated, may hold values from 1 to 3072, 16384 in all
- doc_order: int32 [256], replicated, may hold values from 0 to 255, as said below
Outputs:
- scores: float32 [256, 8192], P('ctx', 'mp')
The draws below stay inside these ranges and needn't reach their ends.
Inputs may be any that keep to these rules, and one draw needn't show every extreme that they name: The lengths sum to 16384; the largest is exactly 3072. `doc_order`: each document appears exactly once; document 0 stands in one of the rows 128 to 143.
All inputs are finite; a program needn't handle non-finite values.
Results may differ from the reference program's by a relative error of at most 0.03.
Values may be sent and summed in bfloat16 or wider, within the bound.
A program may use at most 64 MiB of HBM per device.

```python
import math
import jax
import jax.numpy as jnp
import numpy as np
from jax import lax

D = 5120
FF = 25600
R = 64
TOK_DEV = 1024
DOC_DEV = 16
NQ = 8192
TOKENS = 16384
DOCS = 256
N_MP = 32


def draw_doc_order(key, part):
    key = jax.random.fold_in(key, 5)
    key_perm, key_row = jax.random.split(key)
    shuffled = jax.random.permutation(key_perm, DOCS).astype(jnp.int32)
    target = (DOCS // 2 + jax.random.randint(key_row, (), 0, DOC_DEV)).astype(jnp.int32)
    index = jnp.arange(DOCS, dtype=jnp.int32)
    zero_at = jnp.sum(jnp.where(shuffled == 0, index, 0)).astype(jnp.int32)
    moved = jnp.sum(jnp.where(index == target, shuffled, 0)).astype(jnp.int32)
    result = jnp.where(index == target, 0, jnp.where(index == zero_at, moved, shuffled))
    return result.astype(jnp.int32)


def shard_levels(stream_key, shape, shards, smallest, largest):
    def one(axis_at, parts):
        steps = jax.random.uniform(jax.random.fold_in(jax.random.fold_in(stream_key, 6), axis_at), (parts,), jnp.float32, smallest / len(shards), largest / len(shards))
        return jnp.repeat(jnp.exp(steps), shape[axis_at] // parts).reshape((-1,) + (1,) * (len(shape) - axis_at - 1))

    factor_of = one(*shards[0])
    for cut in shards[1:]:
        factor_of = factor_of * one(*cut)
    return factor_of


def length_profile(count, total, most, slope):
    loads = [(1 << 20) // math.isqrt(grade ** slope) + 1 for grade in range(2, count + 1)]
    surplus, counts = total - most - (count - 1), [1] * (count - 1)
    while surplus > 0:
        candidates = [i for i in range(count - 1) if counts[i] < most]
        pool, remaining = sum([loads[i] for i in candidates]), surplus
        for i in candidates:
            addition = min(most - counts[i], max(1, remaining * loads[i] // pool), surplus)
            counts[i] = counts[i] + addition
            surplus = surplus - addition
    return np.array([most] + counts)


def ragged(rng, number_of, total, limit, slope):
    if number_of == 2:
        one = jax.random.randint(rng, (), max(1, total - limit), min(limit, total - 1) + 1)
        return jnp.stack([one, total - one])
    sizes = jnp.asarray(length_profile(number_of, total, limit, slope), jnp.int32)
    twos = (number_of - 1) // 2
    source_of, sink = sizes[1:1 + 2 * twos:2], sizes[2:2 + 2 * twos:2]
    room = jnp.minimum(source_of - 1, limit - sink)
    passed = jax.random.randint(jax.random.fold_in(rng, 1), (twos,), 0, 1 << 20) % (room + 1)
    sizes = sizes.at[1:1 + 2 * twos:2].set(source_of - passed).at[2:2 + 2 * twos:2].set(sink + passed)
    return sizes[jax.random.permutation(jax.random.fold_in(rng, 2), number_of)]


def gaussian(rng, shape, spread, limit, cuts=(), kind=jnp.bfloat16):
    array = jax.random.normal(rng, shape, jnp.float32) * spread
    if len(cuts) > 0:
        array = shard_levels(rng, shape, cuts, -0.22, 0.18) * array
    return jnp.clip(array, min=-limit, max=limit).astype(kind)


def setup_inputs(seed: int = 0) -> dict:
    seeds = jax.random.split(jax.random.key(seed), 8)
    hidden_act = gaussian(seeds[0], (TOKENS, FF), 1.0, 6.0, ((0, 16), (1, 32)))
    out_grad = gaussian(seeds[1], (TOKENS, D), 1.0, 6.0, ((0, 16), (1, 32)))
    proj_in = gaussian(seeds[2], (FF, R), FF ** -0.5, 0.0390625, ((0, 32),))
    proj_out = gaussian(seeds[3], (D, R), D ** -0.5, 0.078125, ((0, 32),))
    queries = gaussian(seeds[4], (NQ, R * R), (R * R) ** -0.5, 0.09375, ((0, 32),))
    lengths = ragged(seeds[5], DOCS, TOKENS, 3 * TOK_DEV, 2).astype(jnp.int32)
    doc_order = draw_doc_order(jax.random.fold_in(seeds[7], 71), 0)
    return dict(hidden_act=hidden_act, out_grad=out_grad, proj_in=proj_in, proj_out=proj_out, queries=queries, lengths=lengths, doc_order=doc_order)


def grouped_product(data, weight, groups):
    width = data.shape[1] // groups
    total = jnp.zeros((data.shape[0], weight.shape[1]), jnp.float32)
    for group in range(groups):
        part = jnp.dot(data[:, group * width:(group + 1) * width], weight[group * width:(group + 1) * width], preferred_element_type=jnp.float32)
        part = lax.optimization_barrier(part.astype(jnp.bfloat16))
        total = total + part.astype(jnp.float32)
    return total.astype(jnp.bfloat16)

def reference(hidden_act, out_grad, proj_in, proj_out, queries, lengths, doc_order):
    left = grouped_product(hidden_act, proj_in, N_MP)
    right = grouped_product(out_grad, proj_out, N_MP)
    ends = jnp.cumsum(lengths).astype(jnp.int32)
    starts = (ends - lengths).astype(jnp.int32)
    position = jnp.arange(TOKENS, dtype=jnp.int32)
    member = ((position[:, None] >= starts[None, :]) & (position[:, None] < ends[None, :])).astype(jnp.float32)
    weighted = (member[:, :, None] * left.astype(jnp.float32)[:, None, :]).reshape(TOKENS, DOCS * R)
    doc_grad = lax.dot_general(weighted, right.astype(jnp.float32), (((0,), (0,)), ((), ())), precision=lax.Precision.HIGHEST)
    doc_grad = doc_grad.reshape(DOCS, R * R) / jnp.sqrt(lengths.astype(jnp.float32))[:, None]
    ordered = jnp.take(doc_grad, doc_order.astype(jnp.int32), axis=0)
    return lax.dot_general(ordered, queries.astype(jnp.float32), (((1,), (1,)), ((), ())), precision=lax.Precision.HIGHEST)
```

```python
import functools

import jax
import jax.numpy as jnp
from jax import lax
from jax.experimental import pallas as pl
from jax.experimental.pallas import tpu as pltpu
from jax.sharding import PartitionSpec as P

MESH = pl.DeviceIdType.MESH
NZ, NX, NY = 8, 4, 8
NMP, NCTX = NZ * NX, NY * 2
RANK = 64
ZL, XR = RANK // NZ, RANK // NX
F32, BF16 = jnp.float32, jnp.bfloat16


def ring(n):
    return sorted(range(1, n), key=lambda s: (-min(s, n - s), s))


def hops(s, n):
    return min(s, n - s)


Z_OFF, X_OFF, Y_OFF = ring(NZ), ring(NX), ring(NY)
MP_OFF = sorted(
    ((dz, dx) for dz in range(NZ) for dx in range(NX) if dz or dx),
    key=lambda o: (-hops(o[0], NZ) - hops(o[1], NX), o),
)


def kernel(
    hid, grad, pin, pout, qry, lens, order, out,
    vhid, vgrad, vpin, vpout, vq, qp, member, scale,
    lsend, lrecv, l2send, l2recv, rsend, rrecv, r2send, r2recv, gsend, grecv, fsend, frecv,
    load_sem, send_sem, recv_sem,
):
    mp, ctx = lax.axis_index("mp"), lax.axis_index("ctx")
    z, x = mp // NX, lax.rem(mp, NX)
    y, core = ctx // 2, lax.rem(ctx, 2)
    tok = vhid.shape[0]
    half = tok // 2
    quarter = tok // 4
    docs = member.shape[0]
    own = docs // NCTX

    def z_peer(s):
        return (lax.rem(z + s, NZ) * NX + x, ctx)

    def x_peer(s):
        return (z * NX + lax.rem(x + s, NX), ctx)

    def mp_peer(dz, dx):
        return (lax.rem(z + dz, NZ) * NX + lax.rem(x + dx, NX), ctx)

    def ctx_peers():
        for s in Y_OFF:
            for c in (0, 1):
                yield lax.rem(y + s, NY) * 2 + (core if c == 0 else 1 - core)
        yield y * 2 + 1 - core

    loads = [
        pltpu.make_async_copy(grad, vgrad, load_sem.at[0]),
        pltpu.make_async_copy(pout, vpout, load_sem.at[1]),
        pltpu.make_async_copy(pin, vpin, load_sem.at[2]),
        pltpu.make_async_copy(hid.at[pl.ds(0, half)], vhid.at[pl.ds(0, half)], load_sem.at[3]),
        pltpu.make_async_copy(hid.at[pl.ds(half, half)], vhid.at[pl.ds(half, half)], load_sem.at[4]),
        pltpu.make_async_copy(qry, vq, load_sem.at[5]),
    ]
    for load in loads:
        load.start()

    barrier = pltpu.get_barrier_semaphore()
    for dz, dx in MP_OFF:
        pl.semaphore_signal(barrier, inc=1, device_id=mp_peer(dz, dx), device_id_type=MESH)
    for peer in ctx_peers():
        pl.semaphore_signal(barrier, inc=1, device_id=(mp, peer), device_id_type=MESH)

    started = []

    def send(src, dst, phase, device):
        pltpu.make_async_remote_copy(
            src_ref=src, dst_ref=dst, send_sem=send_sem.at[phase], recv_sem=recv_sem.at[phase],
            device_id=device, device_id_type=MESH,
        ).start()

    def arrived(buf, count, phase):
        part = buf.at[pl.ds(0, count)]
        pltpu.make_async_copy(part, part, recv_sem.at[phase]).wait()
        started.append((part, phase))

    loads[0].wait()
    loads[1].wait()
    right = lax.dot_general(vpout[...], vgrad[...], (((0,), (1,)), ((), ())), preferred_element_type=F32)
    right = right.astype(BF16)
    for p in range(NX):
        rsend[p] = right[p * XR:(p + 1) * XR]
    pl.semaphore_wait(barrier, NMP - 1 + NCTX - 1)
    for s in X_OFF:
        send(rsend.at[lax.rem(x + s, NX)], rrecv.at[x], 0, x_peer(s))

    loads[2].wait()
    for b in range(2):
        loads[3 + b].wait()
        left = lax.dot_general(
            vpin[...], vhid[pl.ds(b * half, half), :], (((0,), (1,)), ((), ())), preferred_element_type=F32
        )
        for p in range(NZ):
            rows = left[p * ZL:(p + 1) * ZL]
            slot = jnp.concatenate([rows[:, :quarter], rows[:, quarter:]], axis=0)
            lsend[p, :, b * quarter:(b + 1) * quarter] = slot.astype(BF16)
    for s in Z_OFF:
        send(lsend.at[lax.rem(z + s, NZ)], lrecv.at[z], 1, z_peer(s))
    rrecv[x] = rsend[x]
    lrecv[z] = lsend[z]

    lane = lax.broadcasted_iota(jnp.int32, (docs, docs), 1)
    row = lax.broadcasted_iota(jnp.int32, (docs, docs), 0)
    length = lens[...].astype(F32)
    index = order[...].astype(F32)
    doc = jnp.sum(jnp.where(lane == row, index, 0.0), axis=1, keepdims=True)
    lane_f = lane.astype(F32)
    first = jnp.sum(jnp.where(lane_f < doc, length, 0.0), axis=1, keepdims=True)
    size = jnp.sum(jnp.where(lane_f == doc, length, 0.0), axis=1, keepdims=True)
    scale[...] = jnp.broadcast_to(1.0 / jnp.sqrt(size), scale.shape)
    place = (lax.broadcasted_iota(jnp.int32, (docs, tok), 1) + ctx * tok).astype(F32)
    member[...] = jnp.where((place >= first) & (place < first + size), 1.0, 0.0).astype(BF16)

    arrived(rrecv, NX - 1, 0)
    total = rrecv[0].astype(F32)
    for p in range(1, NX):
        total += rrecv[p].astype(F32)
    r2send[...] = total.astype(BF16)
    for s in Z_OFF:
        send(r2send, r2recv.at[z], 2, z_peer(s))
    r2recv[z] = r2send[...]

    arrived(lrecv, NZ - 1, 1)
    total = lrecv[0].astype(F32)
    for p in range(1, NZ):
        total += lrecv[p].astype(F32)
    l2send[...] = total.astype(BF16)
    for s in X_OFF:
        send(l2send, l2recv.at[x], 3, x_peer(s))
    l2recv[x] = l2send[...]

    loads[5].wait()
    wide = ZL * RANK
    cut = ZL * XR
    to = lax.broadcasted_iota(jnp.int32, (wide, wide), 1)
    at = lax.broadcasted_iota(jnp.int32, (wide, wide), 0)
    source = (to % cut) // XR * RANK + to // cut * XR + to % XR
    moved = jnp.where(at == source, 1.0, 0.0).astype(BF16)
    for p in range(NZ):
        piece = jnp.dot(vq[:, p * wide:(p + 1) * wide], moved, preferred_element_type=F32)
        qp[:, p * wide:(p + 1) * wide] = piece.astype(BF16)

    arrived(l2recv, NX - 1, 3)
    total = l2recv[0].astype(F32)
    for p in range(1, NX):
        total += l2recv[p].astype(F32)
    left = total.astype(BF16).astype(F32)
    arrived(r2recv, NZ - 1, 2)
    total = r2recv[0].astype(F32)
    for p in range(1, NZ):
        total += r2recv[p].astype(F32)
    right = total.astype(BF16).astype(F32)
    sums = jnp.zeros((docs, cut), F32)
    for b in range(2):
        for h in range(2):
            start = b * half + h * quarter
            piece = right[:, start:start + quarter]
            outer = jnp.concatenate(
                [left[h * ZL + i:h * ZL + i + 1, b * quarter:(b + 1) * quarter] * piece for i in range(ZL)], axis=0
            )
            sums += lax.dot_general(
                member[:, start:start + quarter], outer.astype(BF16), (((1,), (1,)), ((), ())),
                preferred_element_type=F32,
            )
    sums = sums.astype(BF16)
    for p in range(NCTX):
        gsend[p] = sums[p * own:(p + 1) * own]
    for peer in ctx_peers():
        send(gsend.at[peer], grecv.at[ctx], 4, (mp, peer))
    grecv[ctx] = gsend[ctx]

    arrived(grecv, NCTX - 1, 4)
    total = grecv[0].astype(F32)
    for p in range(1, NCTX):
        total += grecv[p].astype(F32)
    fsend[...] = (total * scale[pl.ds(ctx * own, own), :]).astype(BF16)
    for dz, dx in MP_OFF:
        send(fsend, frecv.at[mp], 5, mp_peer(dz, dx))
    frecv[mp] = fsend[...]
    arrived(frecv, NMP - 1, 5)

    grads = jnp.concatenate([frecv[p] for p in range(NMP)], axis=1)
    out[...] = lax.dot_general(grads, qp[...], (((1,), (1,)), ((), ())), preferred_element_type=F32)

    for part, phase in started:
        pltpu.make_async_copy(part, part, send_sem.at[phase]).wait()


def local(hidden_act, out_grad, proj_in, proj_out, queries, lengths, doc_order):
    tok, hid = hidden_act.shape
    feat = out_grad.shape[1]
    nq, wide = queries.shape
    docs = lengths.shape[0]
    own = docs // NCTX
    cut = ZL * XR
    anywhere = pl.BlockSpec(memory_space=pl.ANY)
    vmem = pl.BlockSpec(memory_space=pltpu.VMEM)
    scratch = [
        pltpu.VMEM((tok, hid), BF16),
        pltpu.VMEM((tok, feat), BF16),
        pltpu.VMEM((hid, RANK), BF16),
        pltpu.VMEM((feat, RANK), BF16),
        pltpu.VMEM((nq, wide), BF16),
        pltpu.VMEM((nq, wide), BF16),
        pltpu.VMEM((docs, tok), BF16),
        pltpu.VMEM((docs, cut), F32),
        pltpu.VMEM((NZ, 2 * ZL, tok // 2), BF16),
        pltpu.VMEM((NZ, 2 * ZL, tok // 2), BF16),
        pltpu.VMEM((2 * ZL, tok // 2), BF16),
        pltpu.VMEM((NX, 2 * ZL, tok // 2), BF16),
        pltpu.VMEM((NX, XR, tok), BF16),
        pltpu.VMEM((NX, XR, tok), BF16),
        pltpu.VMEM((XR, tok), BF16),
        pltpu.VMEM((NZ, XR, tok), BF16),
        pltpu.VMEM((NCTX, own, cut), BF16),
        pltpu.VMEM((NCTX, own, cut), BF16),
        pltpu.VMEM((own, cut), BF16),
        pltpu.VMEM((NMP, own, cut), BF16),
        pltpu.SemaphoreType.DMA((6,)),
        pltpu.SemaphoreType.DMA((6,)),
        pltpu.SemaphoreType.DMA((6,)),
    ]
    return pl.pallas_call(
        kernel,
        out_shape=jax.ShapeDtypeStruct((own, nq), F32),
        in_specs=[anywhere] * 5 + [vmem] * 2,
        out_specs=vmem,
        scratch_shapes=scratch,
        compiler_params=pltpu.CompilerParams(
            collective_id=0, has_side_effects=True, vmem_limit_bytes=40 * 1024 * 1024
        ),
    )(hidden_act, out_grad, proj_in, proj_out, queries, lengths.reshape(1, docs), doc_order.reshape(1, docs))


def solution(mesh):
    return jax.shard_map(
        local,
        mesh=mesh,
        in_specs=(
            P("ctx", "mp"),
            P("ctx", "mp"),
            P("mp", None),
            P("mp", None),
            P("mp", None),
            P(),
            P(),
        ),
        out_specs=P("ctx", "mp"),
        check_vma=False,
    )
```

```python
import functools

import jax
import jax.numpy as jnp
from jax import lax
from jax.experimental import pallas as pl
from jax.experimental.pallas import tpu as pltpu
from jax.sharding import PartitionSpec as P

MESH = pl.DeviceIdType.MESH
NZ, NX, NY = 8, 4, 8
NMP, NCTX = NZ * NX, NY * 2
RANK = 64
ZL, XR = RANK // NZ, RANK // NX
F32, BF16 = jnp.float32, jnp.bfloat16


def ring(n):
    return sorted(range(1, n), key=lambda s: (-min(s, n - s), s))


def hops(s, n):
    return min(s, n - s)


Z_OFF, X_OFF, Y_OFF = ring(NZ), ring(NX), ring(NY)
MP_OFF = sorted(
    ((dz, dx) for dz in range(NZ) for dx in range(NX) if dz or dx),
    key=lambda o: (-hops(o[0], NZ) - hops(o[1], NX), o),
)


def kernel(
    hid, grad, pin, pout, qry, lens, order, out,
    vhid, vgrad, vpin, vpout, vlens, vorder, vq, qp, member, scale,
    lsend, lrecv, l2send, l2recv, rsend, rrecv, r2send, r2recv, gsend, grecv, fsend, frecv,
    load_sem, send_sem, recv_sem,
):
    mp, ctx = lax.axis_index("mp"), lax.axis_index("ctx")
    z, x = mp // NX, lax.rem(mp, NX)
    y, core = ctx // 2, lax.rem(ctx, 2)
    tok = vhid.shape[1]
    half = tok // 2
    quarter = tok // 4
    docs = member.shape[0]
    own = docs // NCTX

    def z_peer(s):
        return (lax.rem(z + s, NZ) * NX + x, ctx)

    def x_peer(s):
        return (z * NX + lax.rem(x + s, NX), ctx)

    def mp_peer(dz, dx):
        return (lax.rem(z + dz, NZ) * NX + lax.rem(x + dx, NX), ctx)

    def ctx_peers():
        for s in Y_OFF:
            for c in (0, 1):
                yield lax.rem(y + s, NY) * 2 + (core if c == 0 else 1 - core)
        yield y * 2 + 1 - core

    barrier = pltpu.get_barrier_semaphore()
    for s in Z_OFF:
        pl.semaphore_signal(barrier, inc=1, device_id=z_peer(s), device_id_type=MESH)
    for peer in ctx_peers():
        pl.semaphore_signal(barrier, inc=1, device_id=(mp, peer), device_id_type=MESH)
    for s in X_OFF:
        pl.semaphore_signal(barrier, inc=1, device_id=x_peer(s), device_id_type=MESH)

    loads = [
        pltpu.make_async_copy(grad, vgrad, load_sem.at[0]),
        pltpu.make_async_copy(pout, vpout, load_sem.at[1]),
        pltpu.make_async_copy(pin, vpin, load_sem.at[2]),
        pltpu.make_async_copy(hid.at[:, pl.ds(0, half)], vhid.at[:, pl.ds(0, half)], load_sem.at[3]),
        pltpu.make_async_copy(hid.at[:, pl.ds(half, half)], vhid.at[:, pl.ds(half, half)], load_sem.at[4]),
        pltpu.make_async_copy(lens, vlens, load_sem.at[5]),
        pltpu.make_async_copy(order, vorder, load_sem.at[6]),
        pltpu.make_async_copy(qry, vq, load_sem.at[7]),
    ]
    for load in loads:
        load.start()

    started = []

    def send(src, dst, phase, device):
        pltpu.make_async_remote_copy(
            src_ref=src, dst_ref=dst, send_sem=send_sem.at[phase], recv_sem=recv_sem.at[phase],
            device_id=device, device_id_type=MESH,
        ).start()

    def arrived(buf, count, phase):
        part = buf.at[pl.ds(0, count)]
        pltpu.make_async_copy(part, part, recv_sem.at[phase]).wait()
        started.append((part, phase))

    loads[0].wait()
    loads[1].wait()
    right = jnp.dot(vpout[...], vgrad[...], preferred_element_type=F32)
    right = right.astype(BF16)
    for p in range(NX):
        rsend[p] = right[p * XR:(p + 1) * XR]
    loads[2].wait()
    for b in range(2):
        loads[3 + b].wait()
        left = jnp.dot(vpin[...], vhid[:, pl.ds(b * half, half)], preferred_element_type=F32)
        for p in range(NZ):
            rows = left[p * ZL:(p + 1) * ZL]
            slot = jnp.concatenate([rows[:, :quarter], rows[:, quarter:]], axis=0)
            lsend[p, :, b * quarter:(b + 1) * quarter] = slot.astype(BF16)
    pl.semaphore_wait(barrier, NZ - 1 + NX - 1 + NCTX - 1)
    for s in X_OFF:
        send(rsend.at[lax.rem(x + s, NX)], rrecv.at[x], 0, x_peer(s))
    for s in Z_OFF:
        send(lsend.at[lax.rem(z + s, NZ)], lrecv.at[z], 1, z_peer(s))
    rrecv[x] = rsend[x]
    lrecv[z] = lsend[z]

    lane = lax.broadcasted_iota(jnp.int32, (docs, docs), 1)
    row = lax.broadcasted_iota(jnp.int32, (docs, docs), 0)
    loads[5].wait()
    loads[6].wait()
    length = vlens[...].astype(F32).reshape(1, docs)
    index = vorder[...].astype(F32).reshape(1, docs)
    doc = jnp.sum(jnp.where(lane == row, index, 0.0), axis=1, keepdims=True)
    lane_f = lane.astype(F32)
    first = jnp.sum(jnp.where(lane_f < doc, length, 0.0), axis=1, keepdims=True)
    size = jnp.sum(jnp.where(lane_f == doc, length, 0.0), axis=1, keepdims=True)
    scale[...] = jnp.broadcast_to(1.0 / jnp.sqrt(size), scale.shape)
    place = (lax.broadcasted_iota(jnp.int32, (docs, tok), 1) + ctx * tok).astype(F32)
    member[...] = jnp.where((place >= first) & (place < first + size), 1.0, 0.0).astype(BF16)

    arrived(rrecv, NX - 1, 0)
    total = rrecv[0].astype(F32)
    for p in range(1, NX):
        total += rrecv[p].astype(F32)
    r2send[...] = total.astype(BF16)
    for s in Z_OFF:
        send(r2send, r2recv.at[z], 2, z_peer(s))
    r2recv[z] = r2send[...]

    arrived(lrecv, NZ - 1, 1)
    total = lrecv[0].astype(F32)
    for p in range(1, NZ):
        total += lrecv[p].astype(F32)
    l2send[...] = total.astype(BF16)
    for s in X_OFF:
        send(l2send, l2recv.at[x], 3, x_peer(s))
    l2recv[x] = l2send[...]

    loads[7].wait()
    wide = ZL * RANK
    cut = ZL * XR
    to = lax.broadcasted_iota(jnp.int32, (wide, wide), 0)
    at = lax.broadcasted_iota(jnp.int32, (wide, wide), 1)
    source = (to % cut) // XR * RANK + to // cut * XR + to % XR
    moved = jnp.where(at == source, 1.0, 0.0).astype(BF16)
    for p in range(NZ):
        piece = lax.dot_general(
            moved, vq[:, p * wide:(p + 1) * wide], (((1,), (1,)), ((), ())), preferred_element_type=F32
        )
        qp[p * wide:(p + 1) * wide] = piece.astype(BF16)

    arrived(l2recv, NX - 1, 3)
    total = l2recv[0].astype(F32)
    for p in range(1, NX):
        total += l2recv[p].astype(F32)
    left = total.astype(BF16).astype(F32)
    arrived(r2recv, NZ - 1, 2)
    total = r2recv[0].astype(F32)
    for p in range(1, NZ):
        total += r2recv[p].astype(F32)
    right = total.astype(BF16).astype(F32)
    sums = jnp.zeros((docs, cut), F32)
    for b in range(2):
        for h in range(2):
            start = b * half + h * quarter
            piece = right[:, start:start + quarter]
            outer = jnp.concatenate(
                [left[h * ZL + i:h * ZL + i + 1, b * quarter:(b + 1) * quarter] * piece for i in range(ZL)], axis=0
            )
            sums += lax.dot_general(
                member[:, start:start + quarter], outer.astype(BF16), (((1,), (1,)), ((), ())),
                preferred_element_type=F32,
            )
    sums = sums.astype(BF16)
    for p in range(NCTX):
        gsend[p] = sums[p * own:(p + 1) * own]
    for peer in ctx_peers():
        send(gsend.at[peer], grecv.at[ctx], 4, (mp, peer))
    grecv[ctx] = gsend[ctx]

    arrived(grecv, NCTX - 1, 4)
    total = grecv[0].astype(F32)
    for p in range(1, NCTX):
        total += grecv[p].astype(F32)
    fsend[...] = (total * scale[pl.ds(ctx * own, own), :]).astype(BF16)
    for dz, dx in MP_OFF:
        send(fsend, frecv.at[mp], 5, mp_peer(dz, dx))
    frecv[mp] = fsend[...]
    arrived(frecv, NMP - 1, 5)

    grads = jnp.concatenate([frecv[p] for p in range(NMP)], axis=1)
    out[...] = jnp.dot(grads, qp[...], preferred_element_type=F32)

    for part, phase in started:
        pltpu.make_async_copy(part, part, send_sem.at[phase]).wait()


def local(hidden_act, out_grad, proj_in, proj_out, queries, lengths, doc_order):
    tok, hid = hidden_act.shape
    feat = out_grad.shape[1]
    nq, wide = queries.shape
    docs = lengths.shape[0]
    own = docs // NCTX
    cut = ZL * XR
    hbm = pl.BlockSpec(memory_space=pltpu.HBM)
    vmem = pl.BlockSpec(memory_space=pltpu.VMEM)
    scratch = [
        pltpu.VMEM((hid, tok), BF16),
        pltpu.VMEM((feat, tok), BF16),
        pltpu.VMEM((RANK, hid), BF16),
        pltpu.VMEM((RANK, feat), BF16),
        pltpu.VMEM((docs,), jnp.int32),
        pltpu.VMEM((docs,), jnp.int32),
        pltpu.VMEM((nq, wide), BF16),
        pltpu.VMEM((wide, nq), BF16),
        pltpu.VMEM((docs, tok), BF16),
        pltpu.VMEM((docs, cut), F32),
        pltpu.VMEM((NZ, 2 * ZL, tok // 2), BF16),
        pltpu.VMEM((NZ, 2 * ZL, tok // 2), BF16),
        pltpu.VMEM((2 * ZL, tok // 2), BF16),
        pltpu.VMEM((NX, 2 * ZL, tok // 2), BF16),
        pltpu.VMEM((NX, XR, tok), BF16),
        pltpu.VMEM((NX, XR, tok), BF16),
        pltpu.VMEM((XR, tok), BF16),
        pltpu.VMEM((NZ, XR, tok), BF16),
        pltpu.VMEM((NCTX, own, cut), BF16),
        pltpu.VMEM((NCTX, own, cut), BF16),
        pltpu.VMEM((own, cut), BF16),
        pltpu.VMEM((NMP, own, cut), BF16),
        pltpu.SemaphoreType.DMA((8,)),
        pltpu.SemaphoreType.DMA((6,)),
        pltpu.SemaphoreType.DMA((6,)),
    ]
    return pl.pallas_call(
        kernel,
        out_shape=jax.ShapeDtypeStruct((own, nq), F32),
        in_specs=[hbm] * 7,
        out_specs=vmem,
        scratch_shapes=scratch,
        compiler_params=pltpu.CompilerParams(
            collective_id=0, has_side_effects=True, vmem_limit_bytes=60 * 1024 * 1024
        ),
    )(hidden_act.T, out_grad.T, proj_in.T, proj_out.T, queries, lengths, doc_order)


def solution(mesh):
    return jax.shard_map(
        local,
        mesh=mesh,
        in_specs=(
            P("ctx", "mp"),
            P("ctx", "mp"),
            P("mp", None),
            P("mp", None),
            P("mp", None),
            P(),
            P(),
        ),
        out_specs=P("ctx", "mp"),
        check_vma=False,
    )
```

```python
import functools

import jax
import jax.numpy as jnp
from jax import lax
from jax.experimental import pallas as pl
from jax.experimental.pallas import tpu as pltpu
from jax.sharding import PartitionSpec as P

MESH = pl.DeviceIdType.MESH
NZ, NX, NY = 8, 4, 8
NMP, NCTX = NZ * NX, NY * 2
RANK = 64
ZL, XR = RANK // NZ, RANK // NX
F32, BF16 = jnp.float32, jnp.bfloat16


def ring(n):
    return sorted(range(1, n), key=lambda s: (-min(s, n - s), s))


def hops(s, n):
    return min(s, n - s)


Z_OFF, X_OFF, Y_OFF = ring(NZ), ring(NX), ring(NY)
MP_OFF = sorted(
    ((dz, dx) for dz in range(NZ) for dx in range(NX) if dz or dx),
    key=lambda o: (-hops(o[0], NZ) - hops(o[1], NX), o),
)


def kernel(
    hid, grad, pin, pout, qry, lens, order, out,
    vhid, vgrad, vpin, vpout, vlens, vorder, vq, qp, member, scale,
    lsend, lrecv, l2send, l2recv, rsend, rrecv, r2send, r2recv, gsend, grecv, fsend, frecv,
    load_sem, send_sem, recv_sem,
):
    mp, ctx = lax.axis_index("mp"), lax.axis_index("ctx")
    z, x = mp // NX, lax.rem(mp, NX)
    y, core = ctx // 2, lax.rem(ctx, 2)
    odd = lax.rem(z, 2)
    twin = z + 1 - 2 * odd
    tok = vhid.shape[1]
    half = tok // 2
    quarter = tok // 4
    docs = member.shape[0]
    own = docs // NCTX

    def z_peer(s):
        return (lax.rem(z + s, NZ) * NX + x, ctx)

    def x_peer(s):
        return (z * NX + lax.rem(x + s, NX), ctx)

    def pair_peer(s):
        return (twin * NX + lax.rem(x + s, NX), ctx)

    def mp_peer(dz, dx):
        return (lax.rem(z + dz, NZ) * NX + lax.rem(x + dx, NX), ctx)

    def ctx_peers():
        for s in Y_OFF:
            for c in (0, 1):
                yield lax.rem(y + s, NY) * 2 + (core if c == 0 else 1 - core)
        yield y * 2 + 1 - core

    barrier = pltpu.get_barrier_semaphore()
    far, near = [], []
    for s in Z_OFF:
        (far if hops(s, NZ) > 2 else near).append((hops(s, NZ), z_peer(s)))
    for s in Y_OFF:
        for peer in (core, 1 - core):
            device = (mp, lax.rem(y + s, NY) * 2 + peer)
            (far if hops(s, NY) > 2 else near).append((hops(s, NY), device))
    for s in X_OFF:
        near.append((hops(s, NX), x_peer(s)))
        near.append((hops(s, NX) + 1, pair_peer(s)))
    near.append((0, (mp, y * 2 + 1 - core)))

    def greet(devices):
        for _, device in sorted(devices, key=lambda d: -d[0]):
            pl.semaphore_signal(barrier, inc=1, device_id=device, device_id_type=MESH)

    loads = [
        pltpu.make_async_copy(grad, vgrad, load_sem.at[0]),
        pltpu.make_async_copy(pout, vpout, load_sem.at[1]),
        pltpu.make_async_copy(hid.at[:, pl.ds(0, half)], vhid.at[:, pl.ds(0, half)], load_sem.at[3]),
        pltpu.make_async_copy(pin, vpin, load_sem.at[2]),
        pltpu.make_async_copy(hid.at[:, pl.ds(half, half)], vhid.at[:, pl.ds(half, half)], load_sem.at[4]),
        pltpu.make_async_copy(lens, vlens, load_sem.at[5]),
        pltpu.make_async_copy(order, vorder, load_sem.at[6]),
        pltpu.make_async_copy(qry, vq, load_sem.at[7]),
    ]
    greet(far)
    for load in loads[:5]:
        load.start()
    greet(near)

    started = []

    def send(src, dst, phase, device):
        pltpu.make_async_remote_copy(
            src_ref=src, dst_ref=dst, send_sem=send_sem.at[phase], recv_sem=recv_sem.at[phase],
            device_id=device, device_id_type=MESH,
        ).start()

    def arrived(buf, count, phase):
        part = buf.at[pl.ds(0, count)]
        pltpu.make_async_copy(part, part, recv_sem.at[phase]).wait()
        started.append((part, phase))

    loads[0].wait()
    loads[1].wait()
    right = jnp.dot(vpout[...], vgrad[...], preferred_element_type=F32).astype(BF16)
    for p in range(NX):
        for h in range(2):
            rsend[2 * p + h] = right[p * XR:(p + 1) * XR, h * half:(h + 1) * half]

    loads[3].wait()
    for b in range(2):
        loads[2 + 2 * b].wait()
        left = jnp.dot(vpin[...], vhid[:, pl.ds(b * half, half)], preferred_element_type=F32)
        for p in range(NZ):
            rows = left[p * ZL:(p + 1) * ZL]
            slot = jnp.concatenate([rows[:, :quarter], rows[:, quarter:]], axis=0)
            lsend[p, :, b * quarter:(b + 1) * quarter] = slot.astype(BF16)
    pl.semaphore_wait(barrier, NZ - 1 + 2 * (NX - 1) + NCTX - 1)
    for s in X_OFF:
        to = 2 * lax.rem(x + s, NX)
        send(rsend.at[to + 1 - odd], rrecv.at[2 * x + odd], 0, pair_peer(s))
        send(rsend.at[to + odd], rrecv.at[2 * x + odd], 0, x_peer(s))
    send(rsend.at[2 * x + 1 - odd], rrecv.at[2 * x + odd], 0, (twin * NX + x, ctx))
    for s in Z_OFF:
        send(lsend.at[lax.rem(z + s, NZ)], lrecv.at[z], 1, z_peer(s))
    for load in loads[5:]:
        load.start()
    rrecv[2 * x + odd] = rsend[2 * x + odd]
    lrecv[z] = lsend[z]

    lane = lax.broadcasted_iota(jnp.int32, (docs, docs), 1)
    row = lax.broadcasted_iota(jnp.int32, (docs, docs), 0)
    loads[5].wait()
    loads[6].wait()
    length = vlens[...].astype(F32).reshape(1, docs)
    index = vorder[...].astype(F32).reshape(1, docs)
    doc = jnp.sum(jnp.where(lane == row, index, 0.0), axis=1, keepdims=True)
    lane_f = lane.astype(F32)
    first = jnp.sum(jnp.where(lane_f < doc, length, 0.0), axis=1, keepdims=True)
    size = jnp.sum(jnp.where(lane_f == doc, length, 0.0), axis=1, keepdims=True)
    scale[...] = jnp.broadcast_to(1.0 / jnp.sqrt(size), scale.shape)
    place = (lax.broadcasted_iota(jnp.int32, (docs, tok), 1) + ctx * tok).astype(F32)
    member[...] = jnp.where((place >= first) & (place < first + size), 1.0, 0.0).astype(BF16)

    arrived(rrecv, 2 * NX - 1, 0)
    total = rrecv[0].astype(F32)
    for p in range(1, 2 * NX):
        total += rrecv[p].astype(F32)
    r2send[...] = total.astype(BF16)
    for s in Z_OFF:
        send(r2send, r2recv.at[z], 2, z_peer(s))
    r2recv[z] = r2send[...]

    arrived(lrecv, NZ - 1, 1)
    total = lrecv[0].astype(F32)
    for p in range(1, NZ):
        total += lrecv[p].astype(F32)
    l2send[...] = total.astype(BF16)
    for s in X_OFF:
        send(l2send, l2recv.at[x], 3, x_peer(s))
    l2recv[x] = l2send[...]

    loads[7].wait()
    wide = ZL * RANK
    cut = ZL * XR
    to = lax.broadcasted_iota(jnp.int32, (wide, wide), 0)
    at = lax.broadcasted_iota(jnp.int32, (wide, wide), 1)
    source = (to % cut) // XR * RANK + to // cut * XR + to % XR
    moved = jnp.where(at == source, 1.0, 0.0).astype(BF16)
    for p in range(NZ):
        piece = lax.dot_general(
            moved, vq[:, p * wide:(p + 1) * wide], (((1,), (1,)), ((), ())), preferred_element_type=F32
        )
        qp[p * wide:(p + 1) * wide] = piece.astype(BF16)

    arrived(l2recv, NX - 1, 3)
    total = l2recv[0].astype(F32)
    for p in range(1, NX):
        total += l2recv[p].astype(F32)
    left = total.astype(BF16).astype(F32)
    arrived(r2recv, NZ - 1, 2)
    right = []
    for h in range(2):
        total = r2recv[h].astype(F32)
        for p in range(h + 2, NZ, 2):
            total += r2recv[p].astype(F32)
        right.append(total.astype(BF16).astype(F32))
    sums = jnp.zeros((docs, cut), F32)
    for b in range(2):
        for h in range(2):
            start = b * half + h * quarter
            piece = right[b][:, h * quarter:(h + 1) * quarter]
            outer = jnp.concatenate(
                [left[h * ZL + i:h * ZL + i + 1, b * quarter:(b + 1) * quarter] * piece for i in range(ZL)], axis=0
            )
            sums += lax.dot_general(
                member[:, start:start + quarter], outer.astype(BF16), (((1,), (1,)), ((), ())),
                preferred_element_type=F32,
            )
    sums = sums.astype(BF16)
    for p in range(NCTX):
        gsend[p] = sums[p * own:(p + 1) * own]
    for peer in ctx_peers():
        send(gsend.at[peer], grecv.at[ctx], 4, (mp, peer))
    grecv[ctx] = gsend[ctx]

    arrived(grecv, NCTX - 1, 4)
    total = grecv[0].astype(F32)
    for p in range(1, NCTX):
        total += grecv[p].astype(F32)
    fsend[...] = (total * scale[pl.ds(ctx * own, own), :]).astype(BF16)
    for dz, dx in MP_OFF:
        send(fsend, frecv.at[mp], 5, mp_peer(dz, dx))
    frecv[mp] = fsend[...]
    arrived(frecv, NMP - 1, 5)

    grads = jnp.concatenate([frecv[p] for p in range(NMP)], axis=1)
    out[...] = jnp.dot(grads, qp[...], preferred_element_type=F32)

    for part, phase in started:
        pltpu.make_async_copy(part, part, send_sem.at[phase]).wait()


def local(hidden_act, out_grad, proj_in, proj_out, queries, lengths, doc_order):
    tok, hid = hidden_act.shape
    feat = out_grad.shape[1]
    nq, wide = queries.shape
    docs = lengths.shape[0]
    own = docs // NCTX
    cut = ZL * XR
    hbm = pl.BlockSpec(memory_space=pltpu.HBM)
    vmem = pl.BlockSpec(memory_space=pltpu.VMEM)
    scratch = [
        pltpu.VMEM((hid, tok), BF16),
        pltpu.VMEM((feat, tok), BF16),
        pltpu.VMEM((RANK, hid), BF16),
        pltpu.VMEM((RANK, feat), BF16),
        pltpu.VMEM((docs,), jnp.int32),
        pltpu.VMEM((docs,), jnp.int32),
        pltpu.VMEM((nq, wide), BF16),
        pltpu.VMEM((wide, nq), BF16),
        pltpu.VMEM((docs, tok), BF16),
        pltpu.VMEM((docs, cut), F32),
        pltpu.VMEM((NZ, 2 * ZL, tok // 2), BF16),
        pltpu.VMEM((NZ, 2 * ZL, tok // 2), BF16),
        pltpu.VMEM((2 * ZL, tok // 2), BF16),
        pltpu.VMEM((NX, 2 * ZL, tok // 2), BF16),
        pltpu.VMEM((2 * NX, XR, tok // 2), BF16),
        pltpu.VMEM((2 * NX, XR, tok // 2), BF16),
        pltpu.VMEM((XR, tok // 2), BF16),
        pltpu.VMEM((NZ, XR, tok // 2), BF16),
        pltpu.VMEM((NCTX, own, cut), BF16),
        pltpu.VMEM((NCTX, own, cut), BF16),
        pltpu.VMEM((own, cut), BF16),
        pltpu.VMEM((NMP, own, cut), BF16),
        pltpu.SemaphoreType.DMA((8,)),
        pltpu.SemaphoreType.DMA((6,)),
        pltpu.SemaphoreType.DMA((6,)),
    ]
    return pl.pallas_call(
        kernel,
        out_shape=pltpu.VMEM((own, nq), F32),
        in_specs=[hbm] * 7,
        out_specs=vmem,
        scratch_shapes=scratch,
        compiler_params=pltpu.CompilerParams(
            collective_id=0, has_side_effects=True, vmem_limit_bytes=40 * 1024 * 1024
        ),
    )(*[
        pltpu.with_memory_space_constraint(a, pltpu.HBM)
        for a in (hidden_act.T, out_grad.T, proj_in.T, proj_out.T, queries, lengths, doc_order)
    ])


def solution(mesh):
    return jax.shard_map(
        local,
        mesh=mesh,
        in_specs=(
            P("ctx", "mp"),
            P("ctx", "mp"),
            P("mp", None),
            P("mp", None),
            P("mp", None),
            P(),
            P(),
        ),
        out_specs=P("ctx", "mp"),
        check_vma=False,
    )
```

```python
import functools

import jax
import jax.numpy as jnp
from jax import lax
from jax.experimental import pallas as pl
from jax.experimental.pallas import tpu as pltpu
from jax.sharding import PartitionSpec as P

MESH = pl.DeviceIdType.MESH
NZ, NX, NY = 8, 4, 8
NMP, NCTX = NZ * NX, NY * 2
RANK = 64
ZL, XR = RANK // NZ, RANK // NX
F32, BF16 = jnp.float32, jnp.bfloat16


def ring(n):
    return sorted(range(1, n), key=lambda s: (-min(s, n - s), s))


def hops(s, n):
    return min(s, n - s)


Z_OFF, X_OFF, Y_OFF = ring(NZ), ring(NX), ring(NY)
MP_OFF = sorted(
    ((dz, dx) for dz in range(NZ) for dx in range(NX) if dz or dx),
    key=lambda o: (-hops(o[0], NZ) - hops(o[1], NX), o),
)


def kernel(
    hid, grad, pin, pout, qry, lens, order, out,
    vhid, vgrad, vpin, vpout, vlens, vorder, vq, qp, member, scale,
    lsend, lrecv, l2send, l2recv, rsend, rrecv, r2send, r2recv, gsend, grecv, fsend, frecv,
    load_sem, send_sem, recv_sem,
):
    mp, ctx = lax.axis_index("mp"), lax.axis_index("ctx")
    z, x = mp // NX, lax.rem(mp, NX)
    y, core = ctx // 2, lax.rem(ctx, 2)
    odd = lax.rem(z + core, 2)
    twin = lax.rem(z + NZ + 1 - 2 * odd, NZ)
    place_z = lax.rem(z + core, NZ)
    tok = vhid.shape[1]
    half = tok // 2
    quarter = tok // 4
    docs = member.shape[0]
    own = docs // NCTX

    def z_peer(s):
        return (lax.rem(z + s, NZ) * NX + x, ctx)

    def x_peer(s):
        return (z * NX + lax.rem(x + s, NX), ctx)

    def pair_peer(s):
        return (twin * NX + lax.rem(x + s, NX), ctx)

    def mp_peer(dz, dx):
        return (lax.rem(z + dz, NZ) * NX + lax.rem(x + dx, NX), ctx)

    def ctx_peers():
        for s in Y_OFF:
            for c in (0, 1):
                yield lax.rem(y + s, NY) * 2 + (core if c == 0 else 1 - core)
        yield y * 2 + 1 - core

    barrier = pltpu.get_barrier_semaphore()
    far, near = [], []
    for s in Z_OFF:
        (far if hops(s, NZ) > 2 else near).append((hops(s, NZ), z_peer(s)))
    for s in Y_OFF:
        for peer in (core, 1 - core):
            device = (mp, lax.rem(y + s, NY) * 2 + peer)
            (far if hops(s, NY) > 2 else near).append((hops(s, NY), device))
    for s in X_OFF:
        near.append((hops(s, NX), x_peer(s)))
        near.append((hops(s, NX) + 1, pair_peer(s)))
    near.append((0, (mp, y * 2 + 1 - core)))

    def greet(devices):
        for _, device in sorted(devices, key=lambda d: -d[0]):
            pl.semaphore_signal(barrier, inc=1, device_id=device, device_id_type=MESH)

    loads = [
        pltpu.make_async_copy(grad, vgrad, load_sem.at[0]),
        pltpu.make_async_copy(pout, vpout, load_sem.at[1]),
        pltpu.make_async_copy(hid.at[:, pl.ds(0, half)], vhid.at[:, pl.ds(0, half)], load_sem.at[3]),
        pltpu.make_async_copy(pin, vpin, load_sem.at[2]),
        pltpu.make_async_copy(hid.at[:, pl.ds(half, half)], vhid.at[:, pl.ds(half, half)], load_sem.at[4]),
        pltpu.make_async_copy(lens, vlens, load_sem.at[5]),
        pltpu.make_async_copy(order, vorder, load_sem.at[6]),
        pltpu.make_async_copy(qry, vq, load_sem.at[7]),
    ]
    greet(far)
    for load in loads[:5]:
        load.start()
    greet(near)

    started = []

    def send(src, dst, phase, device):
        pltpu.make_async_remote_copy(
            src_ref=src, dst_ref=dst, send_sem=send_sem.at[phase], recv_sem=recv_sem.at[phase],
            device_id=device, device_id_type=MESH,
        ).start()

    def arrived(buf, count, phase):
        part = buf.at[pl.ds(0, count)]
        pltpu.make_async_copy(part, part, recv_sem.at[phase]).wait()
        started.append((part, phase))

    loads[0].wait()
    loads[1].wait()
    right = jnp.dot(vpout[...], vgrad[...], preferred_element_type=F32).astype(BF16)
    for p in range(NX):
        for h in range(2):
            rsend[2 * p + h] = right[p * XR:(p + 1) * XR, h * half:(h + 1) * half]

    loads[3].wait()
    for b in range(2):
        loads[2 + 2 * b].wait()
        left = jnp.dot(vpin[...], vhid[:, pl.ds(b * half, half)], preferred_element_type=F32)
        for p in range(NZ):
            rows = left[p * ZL:(p + 1) * ZL]
            slot = jnp.concatenate([rows[:, :quarter], rows[:, quarter:]], axis=0)
            lsend[p, :, b * quarter:(b + 1) * quarter] = slot.astype(BF16)
    pl.semaphore_wait(barrier, NZ - 1 + 2 * (NX - 1) + NCTX - 1)
    for s in X_OFF:
        to = 2 * lax.rem(x + s, NX)
        send(rsend.at[to + 1 - odd], rrecv.at[2 * x + odd], 0, pair_peer(s))
        send(rsend.at[to + odd], rrecv.at[2 * x + odd], 0, x_peer(s))
    send(rsend.at[2 * x + 1 - odd], rrecv.at[2 * x + odd], 0, (twin * NX + x, ctx))
    for s in Z_OFF:
        send(lsend.at[lax.rem(z + s, NZ)], lrecv.at[z], 1, z_peer(s))
    for load in loads[5:]:
        load.start()
    rrecv[2 * x + odd] = rsend[2 * x + odd]
    lrecv[z] = lsend[z]

    lane = lax.broadcasted_iota(jnp.int32, (docs, docs), 1)
    row = lax.broadcasted_iota(jnp.int32, (docs, docs), 0)
    loads[5].wait()
    loads[6].wait()
    length = vlens[...].astype(F32).reshape(1, docs)
    index = vorder[...].astype(F32).reshape(1, docs)
    doc = jnp.sum(jnp.where(lane == row, index, 0.0), axis=1, keepdims=True)
    lane_f = lane.astype(F32)
    first = jnp.sum(jnp.where(lane_f < doc, length, 0.0), axis=1, keepdims=True)
    size = jnp.sum(jnp.where(lane_f == doc, length, 0.0), axis=1, keepdims=True)
    scale[...] = jnp.broadcast_to(1.0 / jnp.sqrt(size), scale.shape)
    place = (lax.broadcasted_iota(jnp.int32, (docs, tok), 1) + ctx * tok).astype(F32)
    member[...] = jnp.where((place >= first) & (place < first + size), 1.0, 0.0).astype(BF16)

    arrived(rrecv, 2 * NX - 1, 0)
    total = rrecv[0].astype(F32)
    for p in range(1, 2 * NX):
        total += rrecv[p].astype(F32)
    r2send[...] = total.astype(BF16)
    for s in Z_OFF:
        send(r2send, r2recv.at[place_z], 2, z_peer(s))
    r2recv[place_z] = r2send[...]

    arrived(lrecv, NZ - 1, 1)
    total = lrecv[0].astype(F32)
    for p in range(1, NZ):
        total += lrecv[p].astype(F32)
    l2send[...] = total.astype(BF16)
    for s in X_OFF:
        send(l2send, l2recv.at[x], 3, x_peer(s))
    l2recv[x] = l2send[...]

    loads[7].wait()
    wide = ZL * RANK
    cut = ZL * XR
    to = lax.broadcasted_iota(jnp.int32, (wide, wide), 0)
    at = lax.broadcasted_iota(jnp.int32, (wide, wide), 1)
    source = (to % cut) // XR * RANK + to // cut * XR + to % XR
    moved = jnp.where(at == source, 1.0, 0.0).astype(BF16)
    for p in range(NZ):
        piece = lax.dot_general(
            moved, vq[:, p * wide:(p + 1) * wide], (((1,), (1,)), ((), ())), preferred_element_type=F32
        )
        qp[p * wide:(p + 1) * wide] = piece.astype(BF16)

    arrived(l2recv, NX - 1, 3)
    total = l2recv[0].astype(F32)
    for p in range(1, NX):
        total += l2recv[p].astype(F32)
    left = total.astype(BF16).astype(F32)
    arrived(r2recv, NZ - 1, 2)
    right = []
    for h in range(2):
        total = r2recv[h].astype(F32)
        for p in range(h + 2, NZ, 2):
            total += r2recv[p].astype(F32)
        right.append(total.astype(BF16).astype(F32))
    sums = jnp.zeros((docs, cut), F32)
    for b in range(2):
        for h in range(2):
            start = b * half + h * quarter
            piece = right[b][:, h * quarter:(h + 1) * quarter]
            outer = jnp.concatenate(
                [left[h * ZL + i:h * ZL + i + 1, b * quarter:(b + 1) * quarter] * piece for i in range(ZL)], axis=0
            )
            sums += lax.dot_general(
                member[:, start:start + quarter], outer.astype(BF16), (((1,), (1,)), ((), ())),
                preferred_element_type=F32,
            )
    sums = sums.astype(BF16)
    for p in range(NCTX):
        gsend[p] = sums[p * own:(p + 1) * own]
    for peer in ctx_peers():
        send(gsend.at[peer], grecv.at[ctx], 4, (mp, peer))
    grecv[ctx] = gsend[ctx]

    arrived(grecv, NCTX - 1, 4)
    total = grecv[0].astype(F32)
    for p in range(1, NCTX):
        total += grecv[p].astype(F32)
    fsend[...] = (total * scale[pl.ds(ctx * own, own), :]).astype(BF16)
    for dz, dx in MP_OFF:
        send(fsend, frecv.at[mp], 5, mp_peer(dz, dx))
    frecv[mp] = fsend[...]
    arrived(frecv, NMP - 1, 5)

    grads = jnp.concatenate([frecv[p] for p in range(NMP)], axis=1)
    out[...] = jnp.dot(grads, qp[...], preferred_element_type=F32)

    for part, phase in started:
        pltpu.make_async_copy(part, part, send_sem.at[phase]).wait()


def local(hidden_act, out_grad, proj_in, proj_out, queries, lengths, doc_order):
    tok, hid = hidden_act.shape
    feat = out_grad.shape[1]
    nq, wide = queries.shape
    docs = lengths.shape[0]
    own = docs // NCTX
    cut = ZL * XR
    hbm = pl.BlockSpec(memory_space=pltpu.HBM)
    vmem = pl.BlockSpec(memory_space=pltpu.VMEM)
    scratch = [
        pltpu.VMEM((hid, tok), BF16),
        pltpu.VMEM((feat, tok), BF16),
        pltpu.VMEM((RANK, hid), BF16),
        pltpu.VMEM((RANK, feat), BF16),
        pltpu.VMEM((docs,), jnp.int32),
        pltpu.VMEM((docs,), jnp.int32),
        pltpu.VMEM((nq, wide), BF16),
        pltpu.VMEM((wide, nq), BF16),
        pltpu.VMEM((docs, tok), BF16),
        pltpu.VMEM((docs, cut), F32),
        pltpu.VMEM((NZ, 2 * ZL, tok // 2), BF16),
        pltpu.VMEM((NZ, 2 * ZL, tok // 2), BF16),
        pltpu.VMEM((2 * ZL, tok // 2), BF16),
        pltpu.VMEM((NX, 2 * ZL, tok // 2), BF16),
        pltpu.VMEM((2 * NX, XR, tok // 2), BF16),
        pltpu.VMEM((2 * NX, XR, tok // 2), BF16),
        pltpu.VMEM((XR, tok // 2), BF16),
        pltpu.VMEM((NZ, XR, tok // 2), BF16),
        pltpu.VMEM((NCTX, own, cut), BF16),
        pltpu.VMEM((NCTX, own, cut), BF16),
        pltpu.VMEM((own, cut), BF16),
        pltpu.VMEM((NMP, own, cut), BF16),
        pltpu.SemaphoreType.DMA((8,)),
        pltpu.SemaphoreType.DMA((6,)),
        pltpu.SemaphoreType.DMA((6,)),
    ]
    return pl.pallas_call(
        kernel,
        out_shape=pltpu.VMEM((own, nq), F32),
        in_specs=[hbm] * 7,
        out_specs=vmem,
        scratch_shapes=scratch,
        compiler_params=pltpu.CompilerParams(
            collective_id=0, has_side_effects=True, vmem_limit_bytes=40 * 1024 * 1024
        ),
    )(*[
        pltpu.with_memory_space_constraint(a, pltpu.HBM)
        for a in (hidden_act.T, out_grad.T, proj_in.T, proj_out.T, queries, lengths, doc_order)
    ])


def solution(mesh):
    return jax.shard_map(
        local,
        mesh=mesh,
        in_specs=(
            P("ctx", "mp"),
            P("ctx", "mp"),
            P("mp", None),
            P("mp", None),
            P("mp", None),
            P(),
            P(),
        ),
        out_specs=P("ctx", "mp"),
        check_vma=False,
    )
```

```python
import functools

import jax
import jax.numpy as jnp
from jax import lax
from jax.experimental import pallas as pl
from jax.experimental.pallas import tpu as pltpu
from jax.sharding import PartitionSpec as P

MESH = pl.DeviceIdType.MESH
NZ, NX, NY = 8, 4, 8
NMP, NCTX = NZ * NX, NY * 2
RANK = 64
ZL, XR = RANK // NZ, RANK // NX
F32, BF16 = jnp.float32, jnp.bfloat16


def ring(n):
    return sorted(range(1, n), key=lambda s: (-min(s, n - s), s))


def hops(s, n):
    return min(s, n - s)


Z_OFF, X_OFF, Y_OFF = ring(NZ), ring(NX), ring(NY)
MP_OFF = sorted(
    ((dz, dx) for dz in range(NZ) for dx in range(NX) if dz or dx),
    key=lambda o: (-hops(o[0], NZ) - hops(o[1], NX), o),
)

FAR = sum(hops(dz, NZ) + hops(dx, NX) > 3 for dz, dx in MP_OFF)


def kernel(
    hid, grad, pin, pout, qry, lens, order, out,
    vhid, vgrad, vpin, vpout, vlens, vorder, vq, qp, qs, member, scale,
    lsend, lrecv, l2send, l2recv, rsend, rrecv, r2send, r2recv, gsend, grecv, fsend, frecv,
    load_sem, send_sem, recv_sem,
):
    mp, ctx = lax.axis_index("mp"), lax.axis_index("ctx")
    z, x = mp // NX, lax.rem(mp, NX)
    y, core = ctx // 2, lax.rem(ctx, 2)
    odd = lax.rem(z + core, 2)
    twin = lax.rem(z + NZ + 1 - 2 * odd, NZ)
    place_z = lax.rem(z + core, NZ)
    tok = vhid.shape[1]
    half = tok // 2
    quarter = tok // 4
    docs = member.shape[0]
    own = docs // NCTX

    def z_peer(s):
        return (lax.rem(z + s, NZ) * NX + x, ctx)

    def x_peer(s):
        return (z * NX + lax.rem(x + s, NX), ctx)

    def pair_peer(s):
        return (twin * NX + lax.rem(x + s, NX), ctx)

    def mp_peer(dz, dx):
        return (lax.rem(z + dz, NZ) * NX + lax.rem(x + dx, NX), ctx)

    def ctx_peers():
        for s in Y_OFF:
            for c in (0, 1):
                yield lax.rem(y + s, NY) * 2 + (core if c == 0 else 1 - core)
        yield y * 2 + 1 - core

    barrier = pltpu.get_barrier_semaphore()
    mp_peers = [mp_peer(dz, dx) for dz, dx in MP_OFF]
    sources = [lax.rem(z + NZ - dz, NZ) * NX + lax.rem(x + NX - dx, NX) for dz, dx in MP_OFF] + [mp]
    ctx_all = list(ctx_peers())
    z_peers, x_peers, pair_peers = [z_peer(s) for s in Z_OFF], [x_peer(s) for s in X_OFF], [pair_peer(s) for s in X_OFF]
    far, near = [], []
    for s in Z_OFF:
        (far if hops(s, NZ) > 2 else near).append((hops(s, NZ), z_peer(s)))
    for s in Y_OFF:
        for peer in (core, 1 - core):
            device = (mp, lax.rem(y + s, NY) * 2 + peer)
            (far if hops(s, NY) > 2 else near).append((hops(s, NY), device))
    for s in X_OFF:
        near.append((hops(s, NX), x_peer(s)))
        near.append((hops(s, NX) + 1, pair_peer(s)))
    near.append((0, (mp, y * 2 + 1 - core)))

    def greet(devices):
        for _, device in sorted(devices, key=lambda d: -d[0]):
            pl.semaphore_signal(barrier, inc=1, device_id=device, device_id_type=MESH)

    loads = [
        pltpu.make_async_copy(grad, vgrad, load_sem.at[0]),
        pltpu.make_async_copy(pout, vpout, load_sem.at[1]),
        pltpu.make_async_copy(hid.at[:, pl.ds(0, half)], vhid.at[:, pl.ds(0, half)], load_sem.at[3]),
        pltpu.make_async_copy(pin, vpin, load_sem.at[2]),
        pltpu.make_async_copy(hid.at[:, pl.ds(half, half)], vhid.at[:, pl.ds(half, half)], load_sem.at[4]),
        pltpu.make_async_copy(lens, vlens, load_sem.at[5]),
        pltpu.make_async_copy(order, vorder, load_sem.at[6]),
        pltpu.make_async_copy(qry, vq, load_sem.at[7]),
    ]
    greet(far)
    for load in loads[:5]:
        load.start()
    greet(near)

    started = []

    def send(src, dst, phase, device):
        pltpu.make_async_remote_copy(
            src_ref=src, dst_ref=dst, send_sem=send_sem.at[phase], recv_sem=recv_sem.at[phase],
            device_id=device, device_id_type=MESH,
        ).start()

    def arrived(buf, count, phase):
        part = buf.at[pl.ds(0, count)]
        pltpu.make_async_copy(part, part, recv_sem.at[phase]).wait()
        started.append((part, phase))

    loads[0].wait()
    loads[1].wait()
    right = jnp.dot(vpout[...], vgrad[...], preferred_element_type=F32).astype(BF16)
    for p in range(NX):
        for h in range(2):
            rsend[2 * p + h] = right[p * XR:(p + 1) * XR, h * half:(h + 1) * half]

    loads[3].wait()
    for b in range(2):
        loads[2 + 2 * b].wait()
        left = jnp.dot(vpin[...], vhid[:, pl.ds(b * half, half)], preferred_element_type=F32)
        for p in range(NZ):
            rows = left[p * ZL:(p + 1) * ZL]
            slot = jnp.concatenate([rows[:, :quarter], rows[:, quarter:]], axis=0)
            lsend[p, :, b * quarter:(b + 1) * quarter] = slot.astype(BF16)
    pl.semaphore_wait(barrier, NZ - 1 + 2 * (NX - 1) + NCTX - 1)
    for s in X_OFF:
        to = 2 * lax.rem(x + s, NX)
        send(rsend.at[to + 1 - odd], rrecv.at[2 * x + odd], 0, pair_peer(s))
        send(rsend.at[to + odd], rrecv.at[2 * x + odd], 0, x_peer(s))
    send(rsend.at[2 * x + 1 - odd], rrecv.at[2 * x + odd], 0, (twin * NX + x, ctx))
    for s, peer in zip(Z_OFF, z_peers):
        send(lsend.at[lax.rem(z + s, NZ)], lrecv.at[z], 1, peer)
    for load in loads[5:]:
        load.start()
    rrecv[2 * x + odd] = rsend[2 * x + odd]
    lrecv[z] = lsend[z]

    lane = lax.broadcasted_iota(jnp.int32, (docs, docs), 1)
    row = lax.broadcasted_iota(jnp.int32, (docs, docs), 0)
    loads[5].wait()
    loads[6].wait()
    length = vlens[...].astype(F32).reshape(1, docs)
    index = vorder[...].astype(F32).reshape(1, docs)
    doc = jnp.sum(jnp.where(lane == row, index, 0.0), axis=1, keepdims=True)
    lane_f = lane.astype(F32)
    first = jnp.sum(jnp.where(lane_f < doc, length, 0.0), axis=1, keepdims=True)
    size = jnp.sum(jnp.where(lane_f == doc, length, 0.0), axis=1, keepdims=True)
    scale[...] = jnp.broadcast_to(1.0 / jnp.sqrt(size), scale.shape)
    place = (lax.broadcasted_iota(jnp.int32, (docs, tok), 1) + ctx * tok).astype(F32)
    member[...] = jnp.where((place >= first) & (place < first + size), 1.0, 0.0).astype(BF16)

    arrived(rrecv, 2 * NX - 1, 0)
    total = rrecv[0].astype(F32)
    for p in range(1, 2 * NX):
        total += rrecv[p].astype(F32)
    r2send[...] = total.astype(BF16)
    for peer in z_peers:
        send(r2send, r2recv.at[place_z], 2, peer)
    r2recv[place_z] = r2send[...]

    arrived(lrecv, NZ - 1, 1)
    total = lrecv[0].astype(F32)
    for p in range(1, NZ):
        total += lrecv[p].astype(F32)
    l2send[...] = total.astype(BF16)
    for peer in x_peers:
        send(l2send, l2recv.at[x], 3, peer)
    l2recv[x] = l2send[...]

    cut = ZL * XR
    arrived(l2recv, NX - 1, 3)
    total = l2recv[0].astype(F32)
    for p in range(1, NX):
        total += l2recv[p].astype(F32)
    left = total.astype(BF16).astype(F32)
    arrived(r2recv, NZ - 1, 2)
    right = []
    for h in range(2):
        total = r2recv[h].astype(F32)
        for p in range(h + 2, NZ, 2):
            total += r2recv[p].astype(F32)
        right.append(total.astype(BF16).astype(F32))
    sums = jnp.zeros((docs, cut), F32)
    for b in range(2):
        for h in range(2):
            start = b * half + h * quarter
            piece = right[b][:, h * quarter:(h + 1) * quarter]
            outer = jnp.concatenate(
                [left[h * ZL + i:h * ZL + i + 1, b * quarter:(b + 1) * quarter] * piece for i in range(ZL)], axis=0
            )
            sums += lax.dot_general(
                member[:, start:start + quarter], outer.astype(BF16), (((1,), (1,)), ((), ())),
                preferred_element_type=F32,
            )
    sums = sums.astype(BF16)
    for p in range(NCTX):
        gsend[p] = sums[p * own:(p + 1) * own]
    for peer in ctx_all:
        send(gsend.at[peer], grecv.at[ctx], 4, (mp, peer))
    grecv[ctx] = gsend[ctx]

    arrived(grecv, NCTX - 1, 4)
    total = grecv[0].astype(F32)
    for p in range(1, NCTX):
        total += grecv[p].astype(F32)
    fsend[...] = (total * scale[pl.ds(ctx * own, own), :]).astype(BF16)
    for slot, peer in enumerate(mp_peers):
        send(fsend, frecv.at[slot], 5 if slot < FAR else 6, peer)
    frecv[NMP - 1] = fsend[...]

    loads[7].wait()
    wide = ZL * RANK
    to = lax.broadcasted_iota(jnp.int32, (wide, wide), 0)
    at = lax.broadcasted_iota(jnp.int32, (wide, wide), 1)
    source = (to % cut) // XR * RANK + to // cut * XR + to % XR
    moved = jnp.where(at == source, 1.0, 0.0).astype(BF16)
    for p in range(NZ):
        piece = lax.dot_general(
            moved, vq[:, p * wide:(p + 1) * wide], (((1,), (1,)), ((), ())), preferred_element_type=F32
        )
        qp[p * wide:(p + 1) * wide] = piece.astype(BF16)

    for slot, source in enumerate(sources):
        qs[slot * cut:(slot + 1) * cut] = qp[pl.ds(pl.multiple_of(source * cut, cut), cut), :]

    arrived(frecv.at[pl.ds(FAR, NMP - 1 - FAR)], NMP - 1 - FAR, 6)
    grads = jnp.concatenate([frecv[p] for p in range(FAR, NMP)], axis=1)
    part_near = jnp.dot(grads, qs[FAR * cut:], preferred_element_type=F32)
    arrived(frecv, FAR, 5)
    grads = jnp.concatenate([frecv[p] for p in range(FAR)], axis=1)
    out[...] = part_near + jnp.dot(grads, qs[:FAR * cut], preferred_element_type=F32)

    for part, phase in started:
        pltpu.make_async_copy(part, part, send_sem.at[phase]).wait()


def local(hidden_act, out_grad, proj_in, proj_out, queries, lengths, doc_order):
    tok, hid = hidden_act.shape
    feat = out_grad.shape[1]
    nq, wide = queries.shape
    docs = lengths.shape[0]
    own = docs // NCTX
    cut = ZL * XR
    hbm = pl.BlockSpec(memory_space=pltpu.HBM)
    vmem = pl.BlockSpec(memory_space=pltpu.VMEM)
    scratch = [
        pltpu.VMEM((hid, tok), BF16),
        pltpu.VMEM((feat, tok), BF16),
        pltpu.VMEM((RANK, hid), BF16),
        pltpu.VMEM((RANK, feat), BF16),
        pltpu.VMEM((docs,), jnp.int32),
        pltpu.VMEM((docs,), jnp.int32),
        pltpu.VMEM((nq, wide), BF16),
        pltpu.VMEM((wide, nq), BF16),
        pltpu.VMEM((wide, nq), BF16),
        pltpu.VMEM((docs, tok), BF16),
        pltpu.VMEM((docs, cut), F32),
        pltpu.VMEM((NZ, 2 * ZL, tok // 2), BF16),
        pltpu.VMEM((NZ, 2 * ZL, tok // 2), BF16),
        pltpu.VMEM((2 * ZL, tok // 2), BF16),
        pltpu.VMEM((NX, 2 * ZL, tok // 2), BF16),
        pltpu.VMEM((2 * NX, XR, tok // 2), BF16),
        pltpu.VMEM((2 * NX, XR, tok // 2), BF16),
        pltpu.VMEM((XR, tok // 2), BF16),
        pltpu.VMEM((NZ, XR, tok // 2), BF16),
        pltpu.VMEM((NCTX, own, cut), BF16),
        pltpu.VMEM((NCTX, own, cut), BF16),
        pltpu.VMEM((own, cut), BF16),
        pltpu.VMEM((NMP, own, cut), BF16),
        pltpu.SemaphoreType.DMA((8,)),
        pltpu.SemaphoreType.DMA((7,)),
        pltpu.SemaphoreType.DMA((7,)),
    ]
    return pl.pallas_call(
        kernel,
        out_shape=pltpu.VMEM((own, nq), F32),
        in_specs=[hbm] * 7,
        out_specs=vmem,
        scratch_shapes=scratch,
        compiler_params=pltpu.CompilerParams(
            collective_id=0, has_side_effects=True, vmem_limit_bytes=40 * 1024 * 1024
        ),
    )(*[
        pltpu.with_memory_space_constraint(a, pltpu.HBM)
        for a in (hidden_act.T, out_grad.T, proj_in.T, proj_out.T, queries, lengths, doc_order)
    ])


def solution(mesh):
    return jax.shard_map(
        local,
        mesh=mesh,
        in_specs=(
            P("ctx", "mp"),
            P("ctx", "mp"),
            P("mp", None),
            P("mp", None),
            P("mp", None),
            P(),
            P(),
        ),
        out_specs=P("ctx", "mp"),
        check_vma=False,
    )
```

```python
import functools

import jax
import jax.numpy as jnp
from jax import lax
from jax.experimental import pallas as pl
from jax.experimental.pallas import tpu as pltpu
from jax.sharding import PartitionSpec as P

MESH = pl.DeviceIdType.MESH
NZ, NX, NY = 8, 4, 8
NMP, NCTX = NZ * NX, NY * 2
RANK = 64
ZL, XR = RANK // NZ, RANK // NX
F32, BF16 = jnp.float32, jnp.bfloat16


def ring(n):
    return sorted(range(1, n), key=lambda s: (-min(s, n - s), s))


def hops(s, n):
    return min(s, n - s)


Z_OFF, X_OFF, Y_OFF = ring(NZ), ring(NX), ring(NY)
MP_OFF = sorted(
    ((dz, dx) for dz in range(NZ) for dx in range(NX) if dz or dx),
    key=lambda o: (-hops(o[0], NZ) - hops(o[1], NX), o),
)


def kernel(
    hid, grad, pin, pout, qry, lens, order, out,
    vhid, vgrad, vpin, vpout, vlens, vorder, vq, qp, member, scale,
    lsend, lrecv, l2send, l2recv, rsend, rrecv, r2send, r2recv, gsend, grecv, fsend, frecv,
    load_sem, send_sem, recv_sem,
):
    mp, ctx = lax.axis_index("mp"), lax.axis_index("ctx")
    z, x = mp // NX, lax.rem(mp, NX)
    y, core = ctx // 2, lax.rem(ctx, 2)
    odd = lax.rem(z + core, 2)
    twin = lax.rem(z + NZ + 1 - 2 * odd, NZ)
    place_z = lax.rem(z + core, NZ)
    tok = vhid.shape[1]
    half = tok // 2
    quarter = tok // 4
    docs = member.shape[0]
    own = docs // NCTX

    def z_peer(s):
        return (lax.rem(z + s, NZ) * NX + x, ctx)

    def x_peer(s):
        return (z * NX + lax.rem(x + s, NX), ctx)

    def pair_peer(s):
        return (twin * NX + lax.rem(x + s, NX), ctx)

    def mp_peer(dz, dx):
        return (lax.rem(z + dz, NZ) * NX + lax.rem(x + dx, NX), ctx)

    def ctx_peers():
        for s in Y_OFF:
            for c in (0, 1):
                yield lax.rem(y + s, NY) * 2 + (core if c == 0 else 1 - core)
        yield y * 2 + 1 - core

    barrier = pltpu.get_barrier_semaphore()
    far, near = [], []
    for s in Z_OFF:
        (far if hops(s, NZ) > 2 else near).append((hops(s, NZ), z_peer(s)))
    for s in Y_OFF:
        for peer in (core, 1 - core):
            device = (mp, lax.rem(y + s, NY) * 2 + peer)
            (far if hops(s, NY) > 2 else near).append((hops(s, NY), device))
    for s in X_OFF:
        near.append((hops(s, NX), x_peer(s)))
        near.append((hops(s, NX) + 1, pair_peer(s)))
    near.append((0, (mp, y * 2 + 1 - core)))

    def greet(devices):
        for _, device in sorted(devices, key=lambda d: -d[0]):
            pl.semaphore_signal(barrier, inc=1, device_id=device, device_id_type=MESH)

    loads = [
        pltpu.make_async_copy(grad, vgrad, load_sem.at[0]),
        pltpu.make_async_copy(pout, vpout, load_sem.at[1]),
        pltpu.make_async_copy(hid.at[:, pl.ds(0, half)], vhid.at[:, pl.ds(0, half)], load_sem.at[3]),
        pltpu.make_async_copy(pin, vpin, load_sem.at[2]),
        pltpu.make_async_copy(hid.at[:, pl.ds(half, half)], vhid.at[:, pl.ds(half, half)], load_sem.at[4]),
        pltpu.make_async_copy(lens, vlens, load_sem.at[5]),
        pltpu.make_async_copy(order, vorder, load_sem.at[6]),
        pltpu.make_async_copy(qry, vq, load_sem.at[7]),
    ]
    greet(far + [(9, d) for h, d in near if h == 3])
    for load in loads[:5]:
        load.start()
    greet([n for n in near if n[0] != 3])

    started = []

    def send(src, dst, phase, device):
        pltpu.make_async_remote_copy(
            src_ref=src, dst_ref=dst, send_sem=send_sem.at[phase], recv_sem=recv_sem.at[phase],
            device_id=device, device_id_type=MESH,
        ).start()

    def arrived(buf, count, phase):
        part = buf.at[pl.ds(0, count)]
        pltpu.make_async_copy(part, part, recv_sem.at[phase]).wait()
        started.append((part, phase))

    loads[0].wait()
    loads[1].wait()
    right = jnp.dot(vpout[...], vgrad[...], preferred_element_type=F32).astype(BF16)
    for p in range(NX):
        for h in range(2):
            rsend[2 * p + h] = right[p * XR:(p + 1) * XR, h * half:(h + 1) * half]

    loads[3].wait()
    for b in range(2):
        loads[2 + 2 * b].wait()
        left = jnp.dot(vpin[...], vhid[:, pl.ds(b * half, half)], preferred_element_type=F32)
        for p in range(NZ):
            rows = left[p * ZL:(p + 1) * ZL]
            slot = jnp.concatenate([rows[:, :quarter], rows[:, quarter:]], axis=0)
            lsend[p, :, b * quarter:(b + 1) * quarter] = slot.astype(BF16)
    pl.semaphore_wait(barrier, NZ - 1 + 2 * (NX - 1) + NCTX - 1)
    for s in X_OFF:
        to = 2 * lax.rem(x + s, NX)
        send(rsend.at[to + 1 - odd], rrecv.at[2 * x + odd], 0, pair_peer(s))
        send(rsend.at[to + odd], rrecv.at[2 * x + odd], 0, x_peer(s))
    send(rsend.at[2 * x + 1 - odd], rrecv.at[2 * x + odd], 0, (twin * NX + x, ctx))
    for s in Z_OFF:
        send(lsend.at[lax.rem(z + s, NZ)], lrecv.at[z], 1, z_peer(s))
    for load in loads[5:]:
        load.start()
    rrecv[2 * x + odd] = rsend[2 * x + odd]
    lrecv[z] = lsend[z]

    lane = lax.broadcasted_iota(jnp.int32, (docs, docs), 1)
    row = lax.broadcasted_iota(jnp.int32, (docs, docs), 0)
    loads[5].wait()
    loads[6].wait()
    length = vlens[...].astype(F32).reshape(1, docs)
    index = vorder[...].astype(F32).reshape(1, docs)
    doc = jnp.sum(jnp.where(lane == row, index, 0.0), axis=1, keepdims=True)
    lane_f = lane.astype(F32)
    first = jnp.sum(jnp.where(lane_f < doc, length, 0.0), axis=1, keepdims=True)
    size = jnp.sum(jnp.where(lane_f == doc, length, 0.0), axis=1, keepdims=True)
    scale[...] = jnp.broadcast_to(1.0 / jnp.sqrt(size), scale.shape)
    place = (lax.broadcasted_iota(jnp.int32, (docs, tok), 1) + ctx * tok).astype(F32)
    member[...] = jnp.where((place >= first) & (place < first + size), 1.0, 0.0).astype(BF16)

    arrived(rrecv, 2 * NX - 1, 0)
    total = rrecv[0].astype(F32)
    for p in range(1, 2 * NX):
        total += rrecv[p].astype(F32)
    r2send[...] = total.astype(BF16)
    for s in Z_OFF:
        send(r2send, r2recv.at[place_z], 2, z_peer(s))
    r2recv[place_z] = r2send[...]

    arrived(lrecv, NZ - 1, 1)
    total = lrecv[0].astype(F32)
    for p in range(1, NZ):
        total += lrecv[p].astype(F32)
    l2send[...] = total.astype(BF16)
    for s in X_OFF:
        send(l2send, l2recv.at[x], 3, x_peer(s))
    l2recv[x] = l2send[...]

    loads[7].wait()
    wide = ZL * RANK
    cut = ZL * XR
    to = lax.broadcasted_iota(jnp.int32, (wide, wide), 0)
    at = lax.broadcasted_iota(jnp.int32, (wide, wide), 1)
    source = (to % cut) // XR * RANK + to // cut * XR + to % XR
    moved = jnp.where(at == source, 1.0, 0.0).astype(BF16)
    for p in range(NZ):
        piece = lax.dot_general(
            moved, vq[:, p * wide:(p + 1) * wide], (((1,), (1,)), ((), ())), preferred_element_type=F32
        )
        qp[p * wide:(p + 1) * wide] = piece.astype(BF16)

    arrived(l2recv, NX - 1, 3)
    total = l2recv[0].astype(F32)
    for p in range(1, NX):
        total += l2recv[p].astype(F32)
    left = total.astype(BF16).astype(F32)
    arrived(r2recv, NZ - 1, 2)
    right = []
    for h in range(2):
        total = r2recv[h].astype(F32)
        for p in range(h + 2, NZ, 2):
            total += r2recv[p].astype(F32)
        right.append(total.astype(BF16).astype(F32))
    sums = jnp.zeros((docs, cut), F32)
    for b in range(2):
        for h in range(2):
            start = b * half + h * quarter
            piece = right[b][:, h * quarter:(h + 1) * quarter]
            outer = jnp.concatenate(
                [left[h * ZL + i:h * ZL + i + 1, b * quarter:(b + 1) * quarter] * piece for i in range(ZL)], axis=0
            )
            sums += lax.dot_general(
                member[:, start:start + quarter], outer.astype(BF16), (((1,), (1,)), ((), ())),
                preferred_element_type=F32,
            )
    sums = sums.astype(BF16)
    for p in range(NCTX):
        gsend[p] = sums[p * own:(p + 1) * own]
    for peer in ctx_peers():
        send(gsend.at[peer], grecv.at[ctx], 4, (mp, peer))
    grecv[ctx] = gsend[ctx]

    arrived(grecv, NCTX - 1, 4)
    total = grecv[0].astype(F32)
    for p in range(1, NCTX):
        total += grecv[p].astype(F32)
    fsend[...] = (total * scale[pl.ds(ctx * own, own), :]).astype(BF16)
    for dz, dx in MP_OFF:
        send(fsend, frecv.at[mp], 5, mp_peer(dz, dx))
    frecv[mp] = fsend[...]
    arrived(frecv, NMP - 1, 5)

    grads = jnp.concatenate([frecv[p] for p in range(NMP)], axis=1)
    out[...] = jnp.dot(grads, qp[...], preferred_element_type=F32)

    for part, phase in started:
        pltpu.make_async_copy(part, part, send_sem.at[phase]).wait()


def local(hidden_act, out_grad, proj_in, proj_out, queries, lengths, doc_order):
    tok, hid = hidden_act.shape
    feat = out_grad.shape[1]
    nq, wide = queries.shape
    docs = lengths.shape[0]
    own = docs // NCTX
    cut = ZL * XR
    hbm = pl.BlockSpec(memory_space=pltpu.HBM)
    vmem = pl.BlockSpec(memory_space=pltpu.VMEM)
    scratch = [
        pltpu.VMEM((hid, tok), BF16),
        pltpu.VMEM((feat, tok), BF16),
        pltpu.VMEM((RANK, hid), BF16),
        pltpu.VMEM((RANK, feat), BF16),
        pltpu.VMEM((docs,), jnp.int32),
        pltpu.VMEM((docs,), jnp.int32),
        pltpu.VMEM((nq, wide), BF16),
        pltpu.VMEM((wide, nq), BF16),
        pltpu.VMEM((docs, tok), BF16),
        pltpu.VMEM((docs, cut), F32),
        pltpu.VMEM((NZ, 2 * ZL, tok // 2), BF16),
        pltpu.VMEM((NZ, 2 * ZL, tok // 2), BF16),
        pltpu.VMEM((2 * ZL, tok // 2), BF16),
        pltpu.VMEM((NX, 2 * ZL, tok // 2), BF16),
        pltpu.VMEM((2 * NX, XR, tok // 2), BF16),
        pltpu.VMEM((2 * NX, XR, tok // 2), BF16),
        pltpu.VMEM((XR, tok // 2), BF16),
        pltpu.VMEM((NZ, XR, tok // 2), BF16),
        pltpu.VMEM((NCTX, own, cut), BF16),
        pltpu.VMEM((NCTX, own, cut), BF16),
        pltpu.VMEM((own, cut), BF16),
        pltpu.VMEM((NMP, own, cut), BF16),
        pltpu.SemaphoreType.DMA((8,)),
        pltpu.SemaphoreType.DMA((6,)),
        pltpu.SemaphoreType.DMA((6,)),
    ]
    return pl.pallas_call(
        kernel,
        out_shape=pltpu.VMEM((own, nq), F32),
        in_specs=[hbm] * 7,
        out_specs=vmem,
        scratch_shapes=scratch,
        compiler_params=pltpu.CompilerParams(
            collective_id=0, has_side_effects=True, vmem_limit_bytes=40 * 1024 * 1024
        ),
    )(*[
        pltpu.with_memory_space_constraint(a, pltpu.HBM)
        for a in (hidden_act.T, out_grad.T, proj_in.T, proj_out.T, queries, lengths, doc_order)
    ])


def solution(mesh):
    return jax.shard_map(
        local,
        mesh=mesh,
        in_specs=(
            P("ctx", "mp"),
            P("ctx", "mp"),
            P("mp", None),
            P("mp", None),
            P("mp", None),
            P(),
            P(),
        ),
        out_specs=P("ctx", "mp"),
        check_vma=False,
    )
```

```python
import functools

import jax
import jax.numpy as jnp
from jax import lax
from jax.experimental import pallas as pl
from jax.experimental.pallas import tpu as pltpu
from jax.sharding import PartitionSpec as P

MESH = pl.DeviceIdType.MESH
NZ, NX, NY = 8, 4, 8
NMP, NCTX = NZ * NX, NY * 2
RANK = 64
ZL, XR = RANK // NZ, RANK // NX
F32, BF16 = jnp.float32, jnp.bfloat16


def ring(n):
    return sorted(range(1, n), key=lambda s: (-min(s, n - s), s))


def hops(s, n):
    return min(s, n - s)


Z_OFF, X_OFF, Y_OFF = ring(NZ), ring(NX), ring(NY)
MP_OFF = sorted(
    ((dz, dx) for dz in range(NZ) for dx in range(NX) if dz or dx),
    key=lambda o: (-hops(o[0], NZ) - hops(o[1], NX), o),
)

FAR = sum(hops(dz, NZ) + hops(dx, NX) > 4 for dz, dx in MP_OFF)


def kernel(
    hid, grad, pin, pout, qry, lens, order, out,
    vhid, vgrad, vpin, vpout, vlens, vorder, vq, qp, qs, member, scale,
    lsend, lrecv, l2send, l2recv, rsend, rrecv, r2send, r2recv, gsend, grecv, fsend, frecv,
    load_sem, send_sem, recv_sem,
):
    mp, ctx = lax.axis_index("mp"), lax.axis_index("ctx")
    z, x = mp // NX, lax.rem(mp, NX)
    y, core = ctx // 2, lax.rem(ctx, 2)
    odd = lax.rem(z + core, 2)
    twin = lax.rem(z + NZ + 1 - 2 * odd, NZ)
    place_z = lax.rem(z + core, NZ)
    tok = vhid.shape[1]
    half = tok // 2
    quarter = tok // 4
    docs = member.shape[0]
    own = docs // NCTX

    def z_peer(s):
        return (lax.rem(z + s, NZ) * NX + x, ctx)

    def x_peer(s):
        return (z * NX + lax.rem(x + s, NX), ctx)

    def pair_peer(s):
        return (twin * NX + lax.rem(x + s, NX), ctx)

    def mp_peer(dz, dx):
        return (lax.rem(z + dz, NZ) * NX + lax.rem(x + dx, NX), ctx)

    def ctx_peers():
        for s in Y_OFF:
            for c in (0, 1):
                yield lax.rem(y + s, NY) * 2 + (core if c == 0 else 1 - core)
        yield y * 2 + 1 - core

    barrier = pltpu.get_barrier_semaphore()
    mp_peers = [mp_peer(dz, dx) for dz, dx in MP_OFF]
    sources = [lax.rem(z + NZ - dz, NZ) * NX + lax.rem(x + NX - dx, NX) for dz, dx in MP_OFF] + [mp]
    ctx_all = list(ctx_peers())
    z_peers, x_peers, pair_peers = [z_peer(s) for s in Z_OFF], [x_peer(s) for s in X_OFF], [pair_peer(s) for s in X_OFF]
    far, near = [], []
    for s in Z_OFF:
        (far if hops(s, NZ) > 2 else near).append((hops(s, NZ), z_peer(s)))
    for s in Y_OFF:
        for peer in (core, 1 - core):
            device = (mp, lax.rem(y + s, NY) * 2 + peer)
            (far if hops(s, NY) > 2 else near).append((hops(s, NY), device))
    for s in X_OFF:
        near.append((hops(s, NX), x_peer(s)))
        near.append((hops(s, NX) + 1, pair_peer(s)))
    near.append((0, (mp, y * 2 + 1 - core)))

    def greet(devices):
        for _, device in sorted(devices, key=lambda d: -d[0]):
            pl.semaphore_signal(barrier, inc=1, device_id=device, device_id_type=MESH)

    loads = [
        pltpu.make_async_copy(grad, vgrad, load_sem.at[0]),
        pltpu.make_async_copy(pout, vpout, load_sem.at[1]),
        pltpu.make_async_copy(hid.at[:, pl.ds(0, half)], vhid.at[:, pl.ds(0, half)], load_sem.at[3]),
        pltpu.make_async_copy(pin, vpin, load_sem.at[2]),
        pltpu.make_async_copy(hid.at[:, pl.ds(half, half)], vhid.at[:, pl.ds(half, half)], load_sem.at[4]),
        pltpu.make_async_copy(lens, vlens, load_sem.at[5]),
        pltpu.make_async_copy(order, vorder, load_sem.at[6]),
        pltpu.make_async_copy(qry, vq, load_sem.at[7]),
    ]
    greet(far + [(9, d) for h, d in near if h == 3])
    for load in loads[:5]:
        load.start()
    greet([n for n in near if n[0] != 3])

    started = []

    def send(src, dst, phase, device):
        pltpu.make_async_remote_copy(
            src_ref=src, dst_ref=dst, send_sem=send_sem.at[phase], recv_sem=recv_sem.at[phase],
            device_id=device, device_id_type=MESH,
        ).start()

    def arrived(buf, count, phase):
        part = buf.at[pl.ds(0, count)]
        pltpu.make_async_copy(part, part, recv_sem.at[phase]).wait()
        started.append((part, phase))

    loads[0].wait()
    loads[1].wait()
    right = jnp.dot(vpout[...], vgrad[...], preferred_element_type=F32).astype(BF16)
    for p in range(NX):
        for h in range(2):
            rsend[2 * p + h] = right[p * XR:(p + 1) * XR, h * half:(h + 1) * half]

    loads[3].wait()
    for b in range(2):
        loads[2 + 2 * b].wait()
        left = jnp.dot(vpin[...], vhid[:, pl.ds(b * half, half)], preferred_element_type=F32)
        for p in range(NZ):
            rows = left[p * ZL:(p + 1) * ZL]
            slot = jnp.concatenate([rows[:, :quarter], rows[:, quarter:]], axis=0)
            lsend[p, :, b * quarter:(b + 1) * quarter] = slot.astype(BF16)
    pl.semaphore_wait(barrier, NZ - 1 + 2 * (NX - 1) + NCTX - 1)
    for s in X_OFF:
        to = 2 * lax.rem(x + s, NX)
        send(rsend.at[to + 1 - odd], rrecv.at[2 * x + odd], 0, pair_peer(s))
        send(rsend.at[to + odd], rrecv.at[2 * x + odd], 0, x_peer(s))
    send(rsend.at[2 * x + 1 - odd], rrecv.at[2 * x + odd], 0, (twin * NX + x, ctx))
    for s, peer in zip(Z_OFF, z_peers):
        send(lsend.at[lax.rem(z + s, NZ)], lrecv.at[z], 1, peer)
    for load in loads[5:]:
        load.start()
    rrecv[2 * x + odd] = rsend[2 * x + odd]
    lrecv[z] = lsend[z]

    lane = lax.broadcasted_iota(jnp.int32, (docs, docs), 1)
    row = lax.broadcasted_iota(jnp.int32, (docs, docs), 0)
    loads[5].wait()
    loads[6].wait()
    length = vlens[...].astype(F32).reshape(1, docs)
    index = vorder[...].astype(F32).reshape(1, docs)
    doc = jnp.sum(jnp.where(lane == row, index, 0.0), axis=1, keepdims=True)
    lane_f = lane.astype(F32)
    first = jnp.sum(jnp.where(lane_f < doc, length, 0.0), axis=1, keepdims=True)
    size = jnp.sum(jnp.where(lane_f == doc, length, 0.0), axis=1, keepdims=True)
    scale[...] = jnp.broadcast_to(1.0 / jnp.sqrt(size), scale.shape)
    place = (lax.broadcasted_iota(jnp.int32, (docs, tok), 1) + ctx * tok).astype(F32)
    member[...] = jnp.where((place >= first) & (place < first + size), 1.0, 0.0).astype(BF16)

    arrived(rrecv, 2 * NX - 1, 0)
    total = rrecv[0].astype(F32)
    for p in range(1, 2 * NX):
        total += rrecv[p].astype(F32)
    r2send[...] = total.astype(BF16)
    for peer in z_peers:
        send(r2send, r2recv.at[place_z], 2, peer)
    r2recv[place_z] = r2send[...]

    arrived(lrecv, NZ - 1, 1)
    total = lrecv[0].astype(F32)
    for p in range(1, NZ):
        total += lrecv[p].astype(F32)
    l2send[...] = total.astype(BF16)
    for peer in x_peers:
        send(l2send, l2recv.at[x], 3, peer)
    l2recv[x] = l2send[...]

    cut = ZL * XR
    arrived(l2recv, NX - 1, 3)
    total = l2recv[0].astype(F32)
    for p in range(1, NX):
        total += l2recv[p].astype(F32)
    left = total.astype(BF16).astype(F32)
    arrived(r2recv, NZ - 1, 2)
    right = []
    for h in range(2):
        total = r2recv[h].astype(F32)
        for p in range(h + 2, NZ, 2):
            total += r2recv[p].astype(F32)
        right.append(total.astype(BF16).astype(F32))
    sums = jnp.zeros((docs, cut), F32)
    for b in range(2):
        for h in range(2):
            start = b * half + h * quarter
            piece = right[b][:, h * quarter:(h + 1) * quarter]
            outer = jnp.concatenate(
                [left[h * ZL + i:h * ZL + i + 1, b * quarter:(b + 1) * quarter] * piece for i in range(ZL)], axis=0
            )
            sums += lax.dot_general(
                member[:, start:start + quarter], outer.astype(BF16), (((1,), (1,)), ((), ())),
                preferred_element_type=F32,
            )
    sums = sums.astype(BF16)
    for p in range(NCTX):
        gsend[p] = sums[p * own:(p + 1) * own]
    for peer in ctx_all:
        send(gsend.at[peer], grecv.at[ctx], 4, (mp, peer))
    grecv[ctx] = gsend[ctx]

    arrived(grecv, NCTX - 1, 4)
    total = grecv[0].astype(F32)
    for p in range(1, NCTX):
        total += grecv[p].astype(F32)
    fsend[...] = (total * scale[pl.ds(ctx * own, own), :]).astype(BF16)
    for slot, peer in enumerate(mp_peers):
        send(fsend, frecv.at[slot], 5 if slot < FAR else 6, peer)
    frecv[NMP - 1] = fsend[...]

    loads[7].wait()
    wide = ZL * RANK
    to = lax.broadcasted_iota(jnp.int32, (wide, wide), 0)
    at = lax.broadcasted_iota(jnp.int32, (wide, wide), 1)
    source = (to % cut) // XR * RANK + to // cut * XR + to % XR
    moved = jnp.where(at == source, 1.0, 0.0).astype(BF16)
    for p in range(NZ):
        piece = lax.dot_general(
            moved, vq[:, p * wide:(p + 1) * wide], (((1,), (1,)), ((), ())), preferred_element_type=F32
        )
        qp[p * wide:(p + 1) * wide] = piece.astype(BF16)

    for slot, source in enumerate(sources):
        qs[slot * cut:(slot + 1) * cut] = qp[pl.ds(pl.multiple_of(source * cut, cut), cut), :]

    arrived(frecv.at[pl.ds(FAR, NMP - 1 - FAR)], NMP - 1 - FAR, 6)
    grads = jnp.concatenate([frecv[p] for p in range(FAR, NMP)], axis=1)
    part_near = jnp.dot(grads, qs[FAR * cut:], preferred_element_type=F32)
    arrived(frecv, FAR, 5)
    grads = jnp.concatenate([frecv[p] for p in range(FAR)], axis=1)
    out[...] = part_near + jnp.dot(grads, qs[:FAR * cut], preferred_element_type=F32)

    for part, phase in started:
        pltpu.make_async_copy(part, part, send_sem.at[phase]).wait()


def local(hidden_act, out_grad, proj_in, proj_out, queries, lengths, doc_order):
    tok, hid = hidden_act.shape
    feat = out_grad.shape[1]
    nq, wide = queries.shape
    docs = lengths.shape[0]
    own = docs // NCTX
    cut = ZL * XR
    hbm = pl.BlockSpec(memory_space=pltpu.HBM)
    vmem = pl.BlockSpec(memory_space=pltpu.VMEM)
    scratch = [
        pltpu.VMEM((hid, tok), BF16),
        pltpu.VMEM((feat, tok), BF16),
        pltpu.VMEM((RANK, hid), BF16),
        pltpu.VMEM((RANK, feat), BF16),
        pltpu.VMEM((docs,), jnp.int32),
        pltpu.VMEM((docs,), jnp.int32),
        pltpu.VMEM((nq, wide), BF16),
        pltpu.VMEM((wide, nq), BF16),
        pltpu.VMEM((wide, nq), BF16),
        pltpu.VMEM((docs, tok), BF16),
        pltpu.VMEM((docs, cut), F32),
        pltpu.VMEM((NZ, 2 * ZL, tok // 2), BF16),
        pltpu.VMEM((NZ, 2 * ZL, tok // 2), BF16),
        pltpu.VMEM((2 * ZL, tok // 2), BF16),
        pltpu.VMEM((NX, 2 * ZL, tok // 2), BF16),
        pltpu.VMEM((2 * NX, XR, tok // 2), BF16),
        pltpu.VMEM((2 * NX, XR, tok // 2), BF16),
        pltpu.VMEM((XR, tok // 2), BF16),
        pltpu.VMEM((NZ, XR, tok // 2), BF16),
        pltpu.VMEM((NCTX, own, cut), BF16),
        pltpu.VMEM((NCTX, own, cut), BF16),
        pltpu.VMEM((own, cut), BF16),
        pltpu.VMEM((NMP, own, cut), BF16),
        pltpu.SemaphoreType.DMA((8,)),
        pltpu.SemaphoreType.DMA((7,)),
        pltpu.SemaphoreType.DMA((7,)),
    ]
    return pl.pallas_call(
        kernel,
        out_shape=pltpu.VMEM((own, nq), F32),
        in_specs=[hbm] * 7,
        out_specs=vmem,
        scratch_shapes=scratch,
        compiler_params=pltpu.CompilerParams(
            collective_id=0, has_side_effects=True, vmem_limit_bytes=40 * 1024 * 1024
        ),
    )(*[
        pltpu.with_memory_space_constraint(a, pltpu.HBM)
        for a in (hidden_act.T, out_grad.T, proj_in.T, proj_out.T, queries, lengths, doc_order)
    ])


def solution(mesh):
    return jax.shard_map(
        local,
        mesh=mesh,
        in_specs=(
            P("ctx", "mp"),
            P("ctx", "mp"),
            P("mp", None),
            P("mp", None),
            P("mp", None),
            P(),
            P(),
        ),
        out_specs=P("ctx", "mp"),
        check_vma=False,
    )
```
